128 devices in a mesh: dp: 32 (over y, z_lo, x), grad: 4 (over z_hi, core).
Axes of the slice: x: 4, y: 4, z: 4 (z_hi: 2, z_lo: 2; z = z_hi * 2 + z_lo), core: 2. Of those that a mesh axis runs over, the one named last changes fastest.
Arguments:
- grads: float32 [64, 4, 256, 1024], P(None, 'grad', 'dp'), may hold values from -6 to 6
- basis_slots: bfloat16 [32, 4, 2, 1024, 1024], P('dp', 'grad'), may hold values from -0.1875 to 0.1875
- owners: int32 [64, 2], P('dp'), may hold values from 0 to 3, as said below
- eig_in: float32 [64, 1024], P('dp'), may hold values from 0.1 to 3
- eig_out: float32 [64, 1024], P('dp'), may hold values from 0.1 to 3
Outputs:
- precond: float32 [64, 4, 256, 1024], P(None, 'grad', 'dp')
The draws below stay inside these ranges and needn't reach their ends.
Inputs may be any that keep to these rules, and one draw needn't show every extreme that they name: `owners`: each entry is a grad index; within each group of 2 consecutive modules no grad index owns more than 2 of the group's 2 * 2 bases, and at least one grad index owns exactly 2.
All inputs are finite; a program needn't handle non-finite values.
Results may differ from the reference program's by a relative error of at most 0.0003.
Values may be sent and summed in bfloat16 or wider, within the bound.
No kernel may reach another device: no remote copies, remote signals or barrier semaphores. Data moves between devices by JAX's collectives and lax.ppermute only.
A program may use at most 128 MiB of HBM per device.

```python
import math
import jax
import jax.numpy as jnp
from jax import lax

D = 1024
MOD_DEV = 2
MODULES = 64
SLOTS = 2
N_DP = 32
N_GRAD = 4


def draw_owners(key, part):
    key = jax.random.fold_in(key, 11)
    key_heavy, key_order, key_other = jax.random.split(key, 3)
    count = 2 * MOD_DEV
    heavy = jax.random.randint(key_heavy, (N_DP, 1), 0, N_GRAD)
    scores = jax.random.randint(key_order, (N_DP, count), 0, 1 << 20) * count + jnp.arange(count, dtype=jnp.int32)[None, :]
    ranks = jnp.argsort(jnp.argsort(scores, axis=1, stable=True), axis=1, stable=True)
    other = (heavy + jax.random.randint(key_other, (N_DP, count), 1, N_GRAD)) % N_GRAD
    chosen = jnp.where(ranks < MOD_DEV, heavy, other)
    return chosen.reshape(N_DP * MOD_DEV, 2).astype(jnp.int32)


def block_levels(key, dims, pieces, least, largest):
    level, own = 1.0, jax.random.fold_in(key, 6)
    for axis_at, shards_of in pieces:
        steps = jnp.exp(jax.random.uniform(jax.random.fold_in(own, axis_at), (shards_of,), jnp.float32, least / len(pieces), largest / len(pieces)))
        level = level * jnp.repeat(steps, dims[axis_at] // shards_of).reshape([-1 if axis == axis_at else 1 for axis in range(len(dims))])
    return level


def normal_values(stream_key, extent, spread, bound, cuts=(), held_as=jnp.bfloat16):
    entries = spread * jax.random.normal(stream_key, extent, jnp.float32)
    if cuts:
        entries = entries * block_levels(stream_key, extent, cuts, -0.22, 0.18)
    return jnp.clip(entries, -bound, bound).astype(held_as)


def setup_inputs(seed: int = 0) -> dict:
    seeds = jax.random.split(jax.random.key(seed), 6)
    grads = normal_values(seeds[0], (MODULES, N_GRAD, D // N_GRAD, D), 1.0, 6.0, ((1, 4), (2, 32)), jnp.float32)
    basis_slots = normal_values(seeds[1], (N_DP, N_GRAD, SLOTS, D, D), D ** -0.5, 0.1875, ((0, 32), (1, 4)))
    owners = draw_owners(jax.random.fold_in(seeds[5], 71), 0)
    eig_in = jnp.clip(jnp.exp(math.log(3.0) - 3.4011974 * jax.random.uniform(seeds[3], (MODULES, D), jnp.float32) ** block_levels(seeds[3], (MODULES, D), ((0, 32),), -0.2, 0.2)), 0.1, 3.0)
    eig_out = jnp.clip(jnp.exp(math.log(3.0) - 3.4011974 * jax.random.uniform(seeds[4], (MODULES, D), jnp.float32) ** block_levels(seeds[4], (MODULES, D), ((0, 32),), -0.2, 0.2)), 0.1, 3.0)
    return dict(grads=grads, basis_slots=basis_slots, owners=owners, eig_in=eig_in, eig_out=eig_out)


def precondition_one(grad_matrix, basis_a, basis_g, eig_a, eig_g):
    high = lax.Precision.HIGHEST
    rotated = jnp.dot(grad_matrix, basis_a, precision=high)
    eigen_grad = jnp.dot(basis_g.T, rotated, precision=high)
    scaled = eigen_grad / (eig_g[:, None] * eig_a[None, :] + 0.1)
    back_in = jnp.dot(scaled, basis_a.T, precision=high)
    return jnp.dot(basis_g, back_in, precision=high)


def reference(grads, basis_slots, owners, eig_in, eig_out):
    whole = grads.reshape(MODULES, D, D)
    flat = owners.reshape(N_DP, 2 * MOD_DEV)
    order = jnp.arange(2 * MOD_DEV, dtype=jnp.int32)
    same = flat[:, :, None] == flat[:, None, :]
    earlier = order[None, :] < order[:, None]
    slots = jnp.sum((same & earlier[None]).astype(jnp.int32), axis=2).reshape(MODULES, 2)

    def one_module(index):
        group = index // MOD_DEV
        basis_a = basis_slots[group, owners[index, 0], slots[index, 0]].astype(jnp.float32)
        basis_g = basis_slots[group, owners[index, 1], slots[index, 1]].astype(jnp.float32)
        return precondition_one(whole[index], basis_a, basis_g, eig_in[index], eig_out[index])

    result = lax.map(one_module, jnp.arange(MODULES, dtype=jnp.int32))
    return result.reshape(MODULES, N_GRAD, D // N_GRAD, D)
```

```python
import functools

import jax
import jax.numpy as jnp
from jax import lax
from jax.experimental import pallas as pl
from jax.experimental.pallas import tpu as pltpu
from jax.sharding import Mesh, PartitionSpec as P

D = 1024
HALF = 512
WIDE = D + 128
VMEM_LIMIT = 50 * 1024 * 1024
F32 = jnp.float32
BF16 = jnp.bfloat16
I16 = jnp.int16
ANY = pl.BlockSpec(memory_space=pl.ANY)
VMEM = pl.BlockSpec(memory_space=pltpu.VMEM)
SMEM = pl.BlockSpec(memory_space=pltpu.SMEM)
CORE_SWAP = [(0, 1), (1, 0)]


def params(**kw):
    return pltpu.CompilerParams(vmem_limit_bytes=VMEM_LIMIT, **kw)


def basis_of(owners, module, side):
    flat = [owners[0, 0], owners[0, 1], owners[1, 0], owners[1, 1]]
    slot = []
    for k in range(4):
        total = jnp.int32(0)
        for j in range(k):
            total = total + (flat[j] == flat[k]).astype(jnp.int32)
        slot.append(total)
    first = module == 0
    owner = jnp.where(first, flat[side], flat[2 + side])
    return owner, jnp.where(first, slot[side], slot[2 + side])


def split(x):
    high = x.astype(BF16)
    return high, (x - high.astype(F32)).astype(BF16)


def quantize(x):
    most = jnp.maximum(jnp.max(jnp.abs(x), axis=1, keepdims=True), 1e-25)
    step = most * (1.0 / 32700.0)
    exponent = jnp.floor(jnp.log2(step))
    mantissa = jnp.clip(jnp.ceil(step * jnp.exp2(14.0 - exponent)), 1.0, 32767.0)
    scale = mantissa * jnp.exp2(exponent - 14.0)
    whole = jnp.clip(jnp.round(x * (1.0 / scale)), -32767.0, 32767.0)
    lane = lax.broadcasted_iota(jnp.int32, (x.shape[0], 128), 1)
    tail = jnp.where(lane < 64, exponent, mantissa)
    return whole.astype(jnp.int32).astype(I16), tail.astype(jnp.int32).astype(I16)


def scale_of(tail):
    tail = tail.astype(jnp.int32).astype(F32)
    return tail[:, 64:65] * jnp.exp2(tail[:, 0:1] - 14.0)


def quantize_kernel(x_ref, out_ref):
    whole, tail = quantize(x_ref[...])
    out_ref[:, :D] = whole
    out_ref[:, D:] = tail


def quantize_rows(x):
    rows = x.shape[0]
    return pl.pallas_call(
        quantize_kernel,
        grid=(4,),
        in_specs=[pl.BlockSpec((rows // 4, D), lambda i: (i, 0))],
        out_specs=pl.BlockSpec((rows // 4, WIDE), lambda i: (i, 0)),
        out_shape=jax.ShapeDtypeStruct((rows, WIDE), I16),
        compiler_params=params(),
        cost_estimate=pl.CostEstimate(flops=0, bytes_accessed=rows * D * 6, transcendentals=0),
        name="quantize",
    )(x)


def restore_kernel(x_ref, out_ref):
    out_ref[...] = x_ref[:, :D].astype(jnp.int32).astype(F32) * scale_of(x_ref[:, D:])


def restore_rows(x):
    rows = x.shape[0]
    return pl.pallas_call(
        restore_kernel,
        grid=(4,),
        in_specs=[pl.BlockSpec((rows // 4, WIDE), lambda i: (i, 0))],
        out_specs=pl.BlockSpec((rows // 4, D), lambda i: (i, 0)),
        out_shape=jax.ShapeDtypeStruct((rows, D), F32),
        compiler_params=params(),
        cost_estimate=pl.CostEstimate(flops=0, bytes_accessed=rows * D * 6, transcendentals=0),
        name="restore",
    )(x)


def pick_kernel(owners, slots, other, out_a, out_g, sem):
    chip, core = lax.axis_index("zh"), lax.axis_index("core")
    mine, beside = 2 * chip + core, 2 * chip + 1 - core
    start = pl.multiple_of(core * HALF, HALF)
    for side, out in ((0, out_a), (1, out_g)):
        owner, slot = basis_of(owners, 1 - chip, side)
        for holder, source in ((mine, slots), (beside, other)):

            @pl.when(owner == holder)
            def _():
                if side == 0:
                    part = source.at[slot, pl.ds(start, HALF), :]
                else:
                    part = source.at[slot, :, pl.ds(start, HALF)]
                copy = pltpu.make_async_copy(part, out, sem)
                copy.start()
                copy.wait()


def pick(owners, slots, other):
    return pl.pallas_call(
        pick_kernel,
        in_specs=[SMEM, ANY, ANY],
        out_specs=[ANY, ANY],
        out_shape=[jax.ShapeDtypeStruct((HALF, D), BF16), jax.ShapeDtypeStruct((D, HALF), BF16)],
        scratch_shapes=[pltpu.SemaphoreType.DMA],
        compiler_params=params(),
        name="pick",
    )(owners, slots, other)


def load_rows(owners, slots, other, half, half_beside, out, sem):
    chip, core = lax.axis_index("zh"), lax.axis_index("core")
    mine, beside = 2 * chip + core, 2 * chip + 1 - core
    owner, slot = basis_of(owners, chip, 0)
    for holder, source in ((mine, slots), (beside, other)):

        @pl.when(owner == holder)
        def _():
            copy = pltpu.make_async_copy(source.at[slot], out, sem)
            copy.start()
            copy.wait()

    @pl.when((owner != mine) & (owner != beside))
    def _():
        for part, at in ((half, core), (half_beside, 1 - core)):
            copy = pltpu.make_async_copy(part, out.at[pl.ds(pl.multiple_of(at * HALF, HALF), HALF), :], sem)
            copy.start()
            copy.wait()


def load_columns(owners, slots, other, half, which, out, sem):
    chip, core = lax.axis_index("zh"), lax.axis_index("core")
    mine, beside = 2 * chip + core, 2 * chip + 1 - core
    owner, slot = basis_of(owners, chip, 1)
    start = pl.multiple_of(which * HALF, HALF)
    for holder, source in ((mine, slots), (beside, other)):

        @pl.when(owner == holder)
        def _():
            copy = pltpu.make_async_copy(source.at[slot, :, pl.ds(start, HALF)], out, sem)
            copy.start()
            copy.wait()

    @pl.when((owner != mine) & (owner != beside))
    def _():
        copy = pltpu.make_async_copy(half, out, sem)
        copy.start()
        copy.wait()


def rotate_kernel(owners, rows, rows_beside, slots, other, half, half_beside, high_ref, low_ref, basis, sem):
    core = lax.axis_index("core")
    load_rows(owners, slots, other, half, half_beside, basis, sem)
    for source, at in ((rows, core), (rows_beside, 1 - core)):
        for chip in range(2):
            block = source[...].astype(jnp.int32).astype(F32).reshape(32, 2, 8, WIDE)[:, chip].reshape(256, WIDE)
            scale = block[:, D + 64 : D + 65] * jnp.exp2(block[:, D : D + 1] - 14.0)
            high, low = split(block[:, :D])
            start = pl.multiple_of((2 * chip + at) * 256, 256)
            for col in range(0, D, 256):
                part = basis[:, col : col + 256]
                got = jnp.dot(high, part, preferred_element_type=F32) + jnp.dot(low, part, preferred_element_type=F32)
                got_high, got_low = split((got * scale).T)
                high_ref[col : col + 256, pl.ds(start, 256)] = got_high
                low_ref[col : col + 256, pl.ds(start, 256)] = got_low


def rotate(owners, rows, rows_beside, slots, other, half, half_beside):
    return pl.pallas_call(
        rotate_kernel,
        in_specs=[SMEM, VMEM, VMEM, ANY, ANY, ANY, ANY],
        out_specs=[VMEM, VMEM],
        out_shape=[jax.ShapeDtypeStruct((D, D), BF16)] * 2,
        scratch_shapes=[pltpu.VMEM((D, D), BF16), pltpu.SemaphoreType.DMA],
        compiler_params=params(),
        cost_estimate=pl.CostEstimate(flops=4 * D**3, bytes_accessed=9 * D * D, transcendentals=0),
        name="rotate",
    )(owners, rows, rows_beside, slots, other, half, half_beside)


def eigen_part(which, qg, high_ref, low_ref, eig_in, eig_out, add):
    chip, core = lax.axis_index("zh"), lax.axis_index("core")
    first = pl.multiple_of(core * 256, 256)
    eig_g = eig_out[pl.ds(chip, 1), pl.ds(pl.multiple_of(which * HALF, HALF), HALF)]
    tops = [qg[pl.ds(first, 256), :], qg[pl.ds(first + HALF, 256), :]]
    for row in range(0, D, 256):
        eigen = jnp.dot(high_ref[row : row + 256, :], qg[...], preferred_element_type=F32)
        eigen = eigen + jnp.dot(low_ref[row : row + 256, :], qg[...], preferred_element_type=F32)
        eig_a = jnp.broadcast_to(eig_in[pl.ds(chip, 1), row : row + 256], (128, 256)).T[:, 0:1]
        high, low = split(eigen / (eig_a * eig_g + 0.1))
        for at in range(2):
            got = lax.dot_general(tops[at], high, (((1,), (1,)), ((), ())), preferred_element_type=F32)
            got = got + lax.dot_general(tops[at], low, (((1,), (1,)), ((), ())), preferred_element_type=F32)
            add(at * 256, row, got)


def first_kernel(owners, high_ref, low_ref, eig_in, eig_out, slots, other, half, out_ref, qg, sem):
    core = lax.axis_index("core")
    load_columns(owners, slots, other, half, core, qg, sem)

    def add(row, col, got):
        out_ref[row : row + 256, col : col + 256] = got

    eigen_part(core, qg, high_ref, low_ref, eig_in, eig_out, add)


def first_half(owners, high, low, eig_in, eig_out, slots, other, half):
    return pl.pallas_call(
        first_kernel,
        in_specs=[SMEM, VMEM, VMEM, VMEM, VMEM, ANY, ANY, ANY],
        out_specs=VMEM,
        out_shape=jax.ShapeDtypeStruct((HALF, D), F32),
        scratch_shapes=[pltpu.VMEM((D, HALF), BF16), pltpu.SemaphoreType.DMA],
        compiler_params=params(),
        cost_estimate=pl.CostEstimate(flops=3 * D**3, bytes_accessed=7 * D * D, transcendentals=0),
        name="first_half",
    )(owners, high, low, eig_in, eig_out, slots, other, half)


def second_kernel(owners, high_ref, low_ref, eig_in, eig_out, slots, other, half, so_far, half_a, half_a_beside,
                  out_ref, qg, qa, back, sem):
    core = lax.axis_index("core")
    load_columns(owners, slots, other, half, 1 - core, qg, sem)
    load_rows(owners, slots, other, half_a, half_a_beside, qa, sem)

    def add(row, col, got):
        back[row : row + 256, col : col + 256] = so_far[row : row + 256, col : col + 256] + got

    eigen_part(1 - core, qg, high_ref, low_ref, eig_in, eig_out, add)
    for row in range(0, 256, 128):
        pieces = []
        for at in range(2):
            high, low = split(back[at * 256 + row : at * 256 + row + 128, :])
            got = lax.dot_general(high, qa[...], (((1,), (1,)), ((), ())), preferred_element_type=F32)
            got = got + lax.dot_general(low, qa[...], (((1,), (1,)), ((), ())), preferred_element_type=F32)
            pieces.append(got.reshape(16, 1, 8, D))
        whole, tail = quantize(jnp.concatenate(pieces, axis=1).reshape(256, D))
        out_ref[2 * row : 2 * row + 256, :D] = whole
        out_ref[2 * row : 2 * row + 256, D:] = tail


def second_half(owners, high, low, eig_in, eig_out, slots, other, half, so_far, half_a, half_a_beside):
    return pl.pallas_call(
        second_kernel,
        in_specs=[SMEM, VMEM, VMEM, VMEM, VMEM, ANY, ANY, ANY, VMEM, ANY, ANY],
        out_specs=VMEM,
        out_shape=jax.ShapeDtypeStruct((HALF, WIDE), I16),
        scratch_shapes=[
            pltpu.VMEM((D, HALF), BF16),
            pltpu.VMEM((D, D), BF16),
            pltpu.VMEM((HALF, D), F32),
            pltpu.SemaphoreType.DMA,
        ],
        compiler_params=params(),
        cost_estimate=pl.CostEstimate(flops=5 * D**3, bytes_accessed=10 * D * D, transcendentals=0),
        name="second_half",
    )(owners, high, low, eig_in, eig_out, slots, other, half, so_far, half_a, half_a_beside)


def local(grads, basis_slots, owners, eig_in, eig_out):
    def across(x):
        return lax.ppermute(x, "zh", CORE_SWAP)

    def beside(x):
        return lax.ppermute(x, "core", CORE_SWAP)

    def everywhere(x):
        x = x.reshape(64, 8, WIDE)
        return lax.all_to_all(x, ("dp", "zh"), split_axis=0, concat_axis=0, tiled=True).reshape(HALF, WIDE)

    slots = basis_slots[0, 0]
    other = beside(slots)
    packed = quantize_rows(grads.reshape(HALF, D))
    send_a, send_g = pick(owners, slots, other)
    half_a = across(send_a)
    rows = everywhere(packed)
    half_g = across(send_g)
    rows_beside = beside(rows)
    half_a_beside = beside(half_a)
    high, low = rotate(owners, rows, rows_beside, slots, other, half_a, half_a_beside)
    half_g_beside = beside(half_g)
    so_far = first_half(owners, high, low, eig_in, eig_out, slots, other, half_g)
    out = second_half(
        owners, high, low, eig_in, eig_out, slots, other, half_g_beside, so_far, half_a, half_a_beside
    )
    return restore_rows(everywhere(out)).reshape(64, 1, 8, D)


def solution(mesh):
    fine = Mesh(mesh.devices.reshape(32, 2, 2), ("dp", "zh", "core"))
    grad = ("zh", "core")
    return jax.shard_map(
        local,
        mesh=fine,
        in_specs=(
            P(None, grad, "dp", None),
            P("dp", grad, None, None, None),
            P("dp", None),
            P("dp", None),
            P("dp", None),
        ),
        out_specs=P(None, grad, "dp", None),
        check_vma=False,
    )
```

```python
import jax
import jax.numpy as jnp
from jax import lax
from jax.experimental import pallas as pl
from jax.experimental.pallas import tpu as pltpu
from jax.sharding import Mesh, PartitionSpec as P

D = 1024
HALF = 512
QUARTER = 256
LEAD = HALF + QUARTER
WIDE = D + 128
F32 = jnp.float32
BF16 = jnp.bfloat16
I16 = jnp.int16
ANY = pl.BlockSpec(memory_space=pl.ANY)
HBM = pl.BlockSpec(memory_space=pltpu.HBM)
VMEM = pl.BlockSpec(memory_space=pltpu.VMEM)
SMEM = pl.BlockSpec(memory_space=pltpu.SMEM)
CORE_SWAP = [(0, 1), (1, 0)]


def params(mebibytes):
    return pltpu.CompilerParams(vmem_limit_bytes=mebibytes * 1024 * 1024)


def basis_of(owners, module, side):
    flat = [owners[0, 0], owners[0, 1], owners[1, 0], owners[1, 1]]
    slot = []
    for k in range(4):
        total = jnp.int32(0)
        for j in range(k):
            total = total + (flat[j] == flat[k]).astype(jnp.int32)
        slot.append(total)
    first = module == 0
    owner = jnp.where(first, flat[side], flat[2 + side])
    return owner, jnp.where(first, slot[side], slot[2 + side])


def split(x):
    high = x.astype(BF16)
    return high, (x - high.astype(F32)).astype(BF16)


def quantize(x):
    most = jnp.maximum(jnp.max(jnp.abs(x), axis=1, keepdims=True), 1e-25)
    step = most * (1.0 / 32700.0)
    exponent = jnp.floor(jnp.log2(step))
    mantissa = jnp.clip(jnp.ceil(step * jnp.exp2(14.0 - exponent)), 1.0, 32767.0)
    scale = mantissa * jnp.exp2(exponent - 14.0)
    whole = jnp.clip(jnp.round(x * (1.0 / scale)), -32767.0, 32767.0)
    lane = lax.broadcasted_iota(jnp.int32, (x.shape[0], 128), 1)
    tail = jnp.where(lane < 64, exponent, mantissa)
    return whole.astype(jnp.int32).astype(I16), tail.astype(jnp.int32).astype(I16)


def scale_of(tail):
    tail = tail.astype(jnp.int32).astype(F32)
    return tail[:, 64:65] * jnp.exp2(tail[:, 0:1] - 14.0)


def quantize_kernel(x_ref, out_ref):
    whole, tail = quantize(x_ref[...])
    out_ref[:, :D] = whole
    out_ref[:, D:] = tail


def quantize_rows(x):
    rows = x.shape[0]
    return pl.pallas_call(
        quantize_kernel,
        grid=(4,),
        in_specs=[pl.BlockSpec((rows // 4, D), lambda i: (i, 0))],
        out_specs=pl.BlockSpec((rows // 4, WIDE), lambda i: (i, 0)),
        out_shape=jax.ShapeDtypeStruct((rows, WIDE), I16),
        compiler_params=params(12),
        cost_estimate=pl.CostEstimate(flops=0, bytes_accessed=rows * D * 6, transcendentals=0),
        name="quantize",
    )(x)


def restore_kernel(x_ref, out_ref):
    out_ref[...] = x_ref[:, :D].astype(jnp.int32).astype(F32) * scale_of(x_ref[:, D:])


def restore_rows(x):
    rows = x.shape[0]
    return pl.pallas_call(
        restore_kernel,
        grid=(4,),
        in_specs=[pl.BlockSpec((rows // 4, WIDE), lambda i: (i, 0))],
        out_specs=pl.BlockSpec((rows // 4, D), lambda i: (i, 0)),
        out_shape=jax.ShapeDtypeStruct((rows, D), F32),
        compiler_params=params(12),
        cost_estimate=pl.CostEstimate(flops=0, bytes_accessed=rows * D * 6, transcendentals=0),
        name="restore",
    )(x)


def place(owners, module, side, chip, core):
    owner, slot = basis_of(owners, module, side)
    return owner == 2 * chip + core, owner == 2 * chip + 1 - core, slot


def columns(ref, start, size):
    return ref.at[:, pl.ds(pl.multiple_of(start, size), size)]


def run_copies(items, sem):
    for act in ("start", "wait"):
        for at, (wanted, source, out) in enumerate(items):

            @pl.when(wanted)
            def _():
                getattr(pltpu.make_async_copy(source, out, sem.at[at]), act)()


def give_kernel(owners, slots, out, sem):
    chip, core = lax.axis_index("zh"), lax.axis_index("core")
    has_a, _, slot_a = place(owners, 1 - chip, 0, chip, core)
    has_g, _, slot_g = place(owners, 1 - chip, 1, chip, core)
    items = [
        (has_a, columns(slots.at[slot_a], (1 - core) * HALF, HALF), out.at[:, :HALF]),
        (has_g, columns(slots.at[slot_g], (1 - core) * QUARTER, QUARTER), out.at[:, HALF:]),
    ]
    run_copies(items, sem)


def give(owners, slots):
    return pl.pallas_call(
        give_kernel,
        in_specs=[SMEM, HBM],
        out_specs=VMEM,
        out_shape=jax.ShapeDtypeStruct((D, LEAD), BF16),
        scratch_shapes=[pltpu.SemaphoreType.DMA((2,))],
        compiler_params=params(8),
        cost_estimate=pl.CostEstimate(flops=0, bytes_accessed=3 * D * D, transcendentals=0),
        name="give",
    )(owners, slots)


def pick_kernel(owners, slots, given, out, sem):
    chip, core = lax.axis_index("zh"), lax.axis_index("core")
    has_a, beside_a, slot_a = place(owners, 1 - chip, 0, chip, core)
    has_g, beside_g, slot_g = place(owners, 1 - chip, 1, chip, core)
    items = [
        (has_a, columns(slots.at[slot_a], core * HALF, HALF), out.at[:, :HALF]),
        (beside_a, given.at[:, :HALF], out.at[:, :HALF]),
        (has_g, columns(slots.at[slot_g], core * QUARTER, QUARTER), out.at[:, HALF:]),
        (beside_g, given.at[:, HALF:], out.at[:, HALF:]),
    ]
    run_copies(items, sem)


def pick(owners, slots, given):
    return pl.pallas_call(
        pick_kernel,
        in_specs=[SMEM, HBM, ANY],
        out_specs=VMEM,
        out_shape=jax.ShapeDtypeStruct((D, LEAD), BF16),
        scratch_shapes=[pltpu.SemaphoreType.DMA((4,))],
        compiler_params=params(8),
        cost_estimate=pl.CostEstimate(flops=0, bytes_accessed=3 * D * D, transcendentals=0),
        name="pick",
    )(owners, slots, given)


def hold_kernel(owners, slots, other, out, out_a, out_g, sem):
    chip, core = lax.axis_index("zh"), lax.axis_index("core")
    has, beside, slot = place(owners, 1 - chip, 1, chip, core)
    items = [(has, columns(slots.at[slot], HALF + core * QUARTER, QUARTER), out)]
    items.append((beside, columns(other.at[slot], HALF + core * QUARTER, QUARTER), out))
    for side, kept in enumerate((out_a, out_g)):
        has, beside, slot = place(owners, chip, side, chip, core)
        items += [(has, slots.at[slot], kept), (beside, other.at[slot], kept)]
    run_copies(items, sem)


def hold(owners, slots, other):
    return pl.pallas_call(
        hold_kernel,
        in_specs=[SMEM, HBM, HBM],
        out_specs=[VMEM] * 3,
        out_shape=[jax.ShapeDtypeStruct((D, QUARTER), BF16)] + [jax.ShapeDtypeStruct((D, D), BF16)] * 2,
        scratch_shapes=[pltpu.SemaphoreType.DMA((6,))],
        compiler_params=params(10),
        cost_estimate=pl.CostEstimate(flops=0, bytes_accessed=12 * D * D, transcendentals=0),
        name="hold",
    )(owners, slots, other)


def gather(owners, side, kept, kept_at, part, part_beside, part_at, size, out):
    chip, core = lax.axis_index("zh"), lax.axis_index("core")
    has, beside, _ = place(owners, chip, side, chip, core)

    @pl.when(has | beside)
    def _():
        out[...] = kept[:, kept_at : kept_at + 2 * size]

    @pl.when(jnp.logical_not(has | beside))
    def _():
        for source, at in ((part, core), (part_beside, 1 - core)):
            out[:, pl.ds(pl.multiple_of(at * size, size), size)] = source[:, part_at : part_at + size]


def rotate(rows, rows_beside, basis, high_ref, low_ref):
    core = lax.axis_index("core")
    for source, at in ((rows, core), (rows_beside, 1 - core)):
        for chip in range(2):
            block = source[...].astype(jnp.int32).astype(F32).reshape(32, 2, 8, WIDE)[:, chip].reshape(256, WIDE)
            scale = block[:, D + 64 : D + 65] * jnp.exp2(block[:, D : D + 1] - 14.0)
            high, low = split(block[:, :D])
            both = jnp.concatenate([high, low], axis=0)
            start = pl.multiple_of((2 * chip + at) * 256, 256)
            got = jnp.dot(both, basis[...], preferred_element_type=F32)
            got_high, got_low = split(((got[:256] + got[256:]) * scale).T)
            high_ref[:, pl.ds(start, 256)] = got_high
            low_ref[:, pl.ds(start, 256)] = got_low


def eigen_part(which, qg, high_ref, low_ref, eig_in, eig_out, add):
    chip, core = lax.axis_index("zh"), lax.axis_index("core")
    first = pl.multiple_of(core * 256, 256)
    eig_g = eig_out[pl.ds(chip, 1), which * HALF : (which + 1) * HALF]
    tops = jnp.concatenate([qg[pl.ds(first, 256), :], qg[pl.ds(first + HALF, 256), :]], axis=0)
    for row in range(0, D, 512):
        both = jnp.concatenate([high_ref[row : row + 512, :], low_ref[row : row + 512, :]], axis=0)
        eigen = jnp.dot(both, qg[...], preferred_element_type=F32)
        eigen = eigen[:512] + eigen[512:]
        eig_a = jnp.broadcast_to(eig_in[pl.ds(chip, 1), row : row + 512], (128, 512)).T[:, 0:1]
        high, low = split(eigen / (eig_a * eig_g + 0.1))
        got = lax.dot_general(tops, high, (((1,), (1,)), ((), ())), preferred_element_type=F32)
        got = got + lax.dot_general(tops, low, (((1,), (1,)), ((), ())), preferred_element_type=F32)
        add(0, row, got)


def begin_kernel(owners, rows, rows_beside, kept_a, kept_g, lead, lead_beside, eig_in, eig_out,
                 high_ref, low_ref, qa, out_ref, qg):
    gather(owners, 0, kept_a, 0, lead, lead_beside, 0, HALF, qa)
    gather(owners, 1, kept_g, 0, lead, lead_beside, HALF, QUARTER, qg)
    rotate(rows, rows_beside, qa, high_ref, low_ref)

    def add(row, col, got):
        out_ref[:, col : col + 512] = got

    eigen_part(0, qg, high_ref, low_ref, eig_in, eig_out, add)


def begin(owners, rows, rows_beside, kept_a, kept_g, lead, lead_beside, eig_in, eig_out):
    return pl.pallas_call(
        begin_kernel,
        in_specs=[SMEM] + [VMEM] * 8,
        out_specs=[VMEM] * 4,
        out_shape=[jax.ShapeDtypeStruct((D, D), BF16)] * 3 + [jax.ShapeDtypeStruct((HALF, D), F32)],
        scratch_shapes=[pltpu.VMEM((D, HALF), BF16)],
        compiler_params=params(24),
        cost_estimate=pl.CostEstimate(flops=7 * D**3, bytes_accessed=20 * D * D, transcendentals=0),
        name="begin",
    )(owners, rows, rows_beside, kept_a, kept_g, lead, lead_beside, eig_in, eig_out)


def finish_kernel(owners, high_ref, low_ref, qa, so_far, kept_g, rest, rest_beside, eig_in, eig_out,
                  out_ref, qg, back, final):
    gather(owners, 1, kept_g, HALF, rest, rest_beside, 0, QUARTER, qg)

    def add(row, col, got):
        back[:, col : col + 512] = so_far[:, col : col + 512] + got

    eigen_part(1, qg, high_ref, low_ref, eig_in, eig_out, add)
    high, low = split(back[...])
    both = jnp.concatenate([high, low], axis=0)
    for col in range(0, D, 512):
        got = lax.dot_general(both, qa[col : col + 512, :], (((1,), (1,)), ((), ())), preferred_element_type=F32)
        final[:, col : col + 512] = got[:HALF] + got[HALF:]
    for row in range(0, 256, 128):
        pieces = [final[at * 256 + row : at * 256 + row + 128, :].reshape(16, 1, 8, D) for at in range(2)]
        whole, tail = quantize(jnp.concatenate(pieces, axis=1).reshape(256, D))
        out_ref[2 * row : 2 * row + 256, :D] = whole
        out_ref[2 * row : 2 * row + 256, D:] = tail


def finish(owners, high, low, qa, so_far, kept_g, rest, rest_beside, eig_in, eig_out):
    return pl.pallas_call(
        finish_kernel,
        in_specs=[SMEM] + [VMEM] * 9,
        out_specs=VMEM,
        out_shape=jax.ShapeDtypeStruct((HALF, WIDE), I16),
        scratch_shapes=[pltpu.VMEM((D, HALF), BF16), pltpu.VMEM((HALF, D), F32), pltpu.VMEM((HALF, D), F32)],
        compiler_params=params(24),
        cost_estimate=pl.CostEstimate(flops=5 * D**3, bytes_accessed=10 * D * D, transcendentals=0),
        name="finish",
    )(owners, high, low, qa, so_far, kept_g, rest, rest_beside, eig_in, eig_out)


def after(x, earlier):
    return lax.optimization_barrier((x, earlier))[0]


def local(grads, basis_slots, owners, eig_in, eig_out):
    def across(x):
        return lax.ppermute(x, "zh", CORE_SWAP)

    def beside(x):
        return lax.ppermute(x, "core", CORE_SWAP)

    def everywhere(x):
        x = x.reshape(64, 8, WIDE)
        return lax.all_to_all(x, ("dp", "zh"), split_axis=0, concat_axis=0, tiled=True).reshape(HALF, WIDE)

    slots = basis_slots[0, 0]
    send = pick(owners, slots, beside(give(owners, slots)))
    lead = across(send)
    other = beside(after(slots, send))
    send_rest, kept_a, kept_g = hold(owners, slots, other)
    rows = everywhere(after(quantize_rows(grads.reshape(HALF, D)), send_rest))
    rest = across(send_rest)
    high, low, qa, so_far = begin(
        owners, rows, beside(rows), kept_a, kept_g, lead, beside(lead), eig_in, eig_out
    )
    rest_beside = beside(after(rest, so_far))
    out = finish(owners, high, low, qa, so_far, kept_g, rest, rest_beside, eig_in, eig_out)
    return restore_rows(everywhere(out)).reshape(64, 1, 8, D)


def solution(mesh):
    fine = Mesh(mesh.devices.reshape(32, 2, 2), ("dp", "zh", "core"))
    grad = ("zh", "core")
    return jax.shard_map(
        local,
        mesh=fine,
        in_specs=(
            P(None, grad, "dp", None),
            P("dp", grad, None, None, None),
            P("dp", None),
            P("dp", None),
            P("dp", None),
        ),
        out_specs=P(None, grad, "dp", None),
        check_vma=False,
    )
```

```python
import jax
import jax.numpy as jnp
from jax import lax
from jax.experimental import pallas as pl
from jax.experimental.pallas import tpu as pltpu
from jax.sharding import Mesh, PartitionSpec as P

D = 1024
HALF = 512
QUARTER = 256
LEAD = HALF + QUARTER
WIDE = D + 128
F32 = jnp.float32
BF16 = jnp.bfloat16
I16 = jnp.int16
ANY = pl.BlockSpec(memory_space=pl.ANY)
HBM = pl.BlockSpec(memory_space=pltpu.HBM)
VMEM = pl.BlockSpec(memory_space=pltpu.VMEM)
SMEM = pl.BlockSpec(memory_space=pltpu.SMEM)
CORE_SWAP = [(0, 1), (1, 0)]


def params(mebibytes):
    return pltpu.CompilerParams(vmem_limit_bytes=mebibytes * 1024 * 1024)


def basis_of(owners, module, side):
    flat = [owners[0, 0], owners[0, 1], owners[1, 0], owners[1, 1]]
    slot = []
    for k in range(4):
        total = jnp.int32(0)
        for j in range(k):
            total = total + (flat[j] == flat[k]).astype(jnp.int32)
        slot.append(total)
    first = module == 0
    owner = jnp.where(first, flat[side], flat[2 + side])
    return owner, jnp.where(first, slot[side], slot[2 + side])


def split(x):
    high = x.astype(BF16)
    return high, (x - high.astype(F32)).astype(BF16)


def quantize(x):
    most = jnp.maximum(jnp.max(jnp.abs(x), axis=1, keepdims=True), 1e-25)
    step = most * (1.0 / 32700.0)
    exponent = jnp.floor(jnp.log2(step))
    mantissa = jnp.clip(jnp.ceil(step * jnp.exp2(14.0 - exponent)), 1.0, 32767.0)
    scale = mantissa * jnp.exp2(exponent - 14.0)
    whole = jnp.clip(jnp.round(x * (1.0 / scale)), -32767.0, 32767.0)
    lane = lax.broadcasted_iota(jnp.int32, (x.shape[0], 128), 1)
    tail = jnp.where(lane < 64, exponent, mantissa)
    return whole.astype(jnp.int32).astype(I16), tail.astype(jnp.int32).astype(I16)


def scale_of(tail):
    tail = tail.astype(jnp.int32).astype(F32)
    return tail[:, 64:65] * jnp.exp2(tail[:, 0:1] - 14.0)


def quantize_kernel(x_ref, out_ref):
    whole, tail = quantize(x_ref[...])
    out_ref[:, :D] = whole
    out_ref[:, D:] = tail


def quantize_rows(x):
    rows = x.shape[0]
    return pl.pallas_call(
        quantize_kernel,
        grid=(4,),
        in_specs=[pl.BlockSpec((rows // 4, D), lambda i: (i, 0))],
        out_specs=pl.BlockSpec((rows // 4, WIDE), lambda i: (i, 0)),
        out_shape=jax.ShapeDtypeStruct((rows, WIDE), I16),
        compiler_params=params(12),
        cost_estimate=pl.CostEstimate(flops=0, bytes_accessed=rows * D * 6, transcendentals=0),
        name="quantize",
    )(x)


def restore_kernel(x_ref, out_ref):
    out_ref[...] = x_ref[:, :D].astype(jnp.int32).astype(F32) * scale_of(x_ref[:, D:])


def restore_rows(x):
    rows = x.shape[0]
    return pl.pallas_call(
        restore_kernel,
        grid=(4,),
        in_specs=[pl.BlockSpec((rows // 4, WIDE), lambda i: (i, 0))],
        out_specs=pl.BlockSpec((rows // 4, D), lambda i: (i, 0)),
        out_shape=jax.ShapeDtypeStruct((rows, D), F32),
        compiler_params=params(12),
        cost_estimate=pl.CostEstimate(flops=0, bytes_accessed=rows * D * 6, transcendentals=0),
        name="restore",
    )(x)


def place(owners, module, side, chip, core):
    owner, slot = basis_of(owners, module, side)
    return owner == 2 * chip + core, owner == 2 * chip + 1 - core, slot


def columns(ref, start, size):
    return ref.at[:, pl.ds(pl.multiple_of(start, size), size)]


def run_copies(items, sem):
    for act in ("start", "wait"):
        for at, (wanted, source, out) in enumerate(items):

            @pl.when(wanted)
            def _():
                getattr(pltpu.make_async_copy(source, out, sem.at[at]), act)()


def give_kernel(owners, slots, out, sem):
    chip, core = lax.axis_index("zh"), lax.axis_index("core")
    has_a, _, slot_a = place(owners, 1 - chip, 0, chip, core)
    has_g, _, slot_g = place(owners, 1 - chip, 1, chip, core)
    items = [
        (has_a, columns(slots.at[slot_a], (1 - core) * HALF, HALF), out.at[:, :HALF]),
        (has_g, columns(slots.at[slot_g], (1 - core) * QUARTER, QUARTER), out.at[:, HALF:]),
    ]
    run_copies(items, sem)


def give(owners, slots):
    return pl.pallas_call(
        give_kernel,
        in_specs=[SMEM, HBM],
        out_specs=VMEM,
        out_shape=jax.ShapeDtypeStruct((D, LEAD), BF16),
        scratch_shapes=[pltpu.SemaphoreType.DMA((2,))],
        compiler_params=params(8),
        cost_estimate=pl.CostEstimate(flops=0, bytes_accessed=3 * D * D, transcendentals=0),
        name="give",
    )(owners, slots)


def pick_kernel(owners, slots, given, out, sem):
    chip, core = lax.axis_index("zh"), lax.axis_index("core")
    has_a, beside_a, slot_a = place(owners, 1 - chip, 0, chip, core)
    has_g, beside_g, slot_g = place(owners, 1 - chip, 1, chip, core)
    items = [
        (has_a, columns(slots.at[slot_a], core * HALF, HALF), out.at[:, :HALF]),
        (beside_a, given.at[:, :HALF], out.at[:, :HALF]),
        (has_g, columns(slots.at[slot_g], core * QUARTER, QUARTER), out.at[:, HALF:]),
        (beside_g, given.at[:, HALF:], out.at[:, HALF:]),
    ]
    run_copies(items, sem)


def pick(owners, slots, given):
    return pl.pallas_call(
        pick_kernel,
        in_specs=[SMEM, HBM, ANY],
        out_specs=VMEM,
        out_shape=jax.ShapeDtypeStruct((D, LEAD), BF16),
        scratch_shapes=[pltpu.SemaphoreType.DMA((4,))],
        compiler_params=params(8),
        cost_estimate=pl.CostEstimate(flops=0, bytes_accessed=3 * D * D, transcendentals=0),
        name="pick",
    )(owners, slots, given)


def rest_kernel(owners, slots, other, out, sem):
    chip, core = lax.axis_index("zh"), lax.axis_index("core")
    has, beside, slot = place(owners, 1 - chip, 1, chip, core)
    items = []
    for wanted, source in ((has, slots), (beside, other)):
        items.append((wanted, columns(source.at[slot], HALF + core * QUARTER, QUARTER), out))
    run_copies(items, sem)


def keep_kernel(owners, slots, other, out_a, out_g, sem):
    chip, core = lax.axis_index("zh"), lax.axis_index("core")
    items = []
    for side, kept in enumerate((out_a, out_g)):
        has, beside, slot = place(owners, chip, side, chip, core)
        items += [(has, slots.at[slot], kept), (beside, other.at[slot], kept)]
    run_copies(items, sem)


def hold(kernel, shapes, owners, slots, other):
    return pl.pallas_call(
        kernel,
        in_specs=[SMEM, HBM, HBM],
        out_specs=[VMEM] * len(shapes),
        out_shape=[jax.ShapeDtypeStruct(shape, BF16) for shape in shapes],
        scratch_shapes=[pltpu.SemaphoreType.DMA((4,))],
        compiler_params=params(10),
        cost_estimate=pl.CostEstimate(flops=0, bytes_accessed=4 * D * D, transcendentals=0),
        name="hold",
    )(owners, slots, other)


def gather(owners, side, kept, kept_at, part, part_beside, part_at, size, out):
    chip, core = lax.axis_index("zh"), lax.axis_index("core")
    has, beside, _ = place(owners, chip, side, chip, core)

    @pl.when(has | beside)
    def _():
        out[...] = kept[:, kept_at : kept_at + 2 * size]

    @pl.when(jnp.logical_not(has | beside))
    def _():
        for source, at in ((part, core), (part_beside, 1 - core)):
            out[:, pl.ds(pl.multiple_of(at * size, size), size)] = source[:, part_at : part_at + size]


def rotate(rows, rows_beside, basis, high_ref, low_ref):
    core = lax.axis_index("core")
    for source, at in ((rows, core), (rows_beside, 1 - core)):
        for chip in range(2):
            block = source[...].astype(jnp.int32).astype(F32).reshape(32, 2, 8, WIDE)[:, chip].reshape(256, WIDE)
            scale = block[:, D + 64 : D + 65] * jnp.exp2(block[:, D : D + 1] - 14.0)
            high, low = split(block[:, :D])
            both = jnp.concatenate([high, low], axis=0)
            start = pl.multiple_of((2 * chip + at) * 256, 256)
            got = jnp.dot(both, basis[...], preferred_element_type=F32)
            got_high, got_low = split(((got[:256] + got[256:]) * scale).T)
            high_ref[:, pl.ds(start, 256)] = got_high
            low_ref[:, pl.ds(start, 256)] = got_low


def eigen_part(which, qg, high_ref, low_ref, eig_in, eig_out, add):
    chip, core = lax.axis_index("zh"), lax.axis_index("core")
    first = pl.multiple_of(core * 256, 256)
    eig_g = eig_out[pl.ds(chip, 1), which * HALF : (which + 1) * HALF]
    tops = jnp.concatenate([qg[pl.ds(first, 256), :], qg[pl.ds(first + HALF, 256), :]], axis=0)
    for row in range(0, D, 512):
        both = jnp.concatenate([high_ref[row : row + 512, :], low_ref[row : row + 512, :]], axis=0)
        eigen = jnp.dot(both, qg[...], preferred_element_type=F32)
        eigen = eigen[:512] + eigen[512:]
        eig_a = jnp.broadcast_to(eig_in[pl.ds(chip, 1), row : row + 512], (128, 512)).T[:, 0:1]
        high, low = split(eigen / (eig_a * eig_g + 0.1))
        got = lax.dot_general(tops, high, (((1,), (1,)), ((), ())), preferred_element_type=F32)
        got = got + lax.dot_general(tops, low, (((1,), (1,)), ((), ())), preferred_element_type=F32)
        add(0, row, got)


def begin_kernel(owners, rows, rows_beside, kept_a, kept_g, lead, lead_beside, eig_in, eig_out,
                 high_ref, low_ref, qa, out_ref, qg):
    gather(owners, 0, kept_a, 0, lead, lead_beside, 0, HALF, qa)
    gather(owners, 1, kept_g, 0, lead, lead_beside, HALF, QUARTER, qg)
    rotate(rows, rows_beside, qa, high_ref, low_ref)

    def add(row, col, got):
        out_ref[:, col : col + 512] = got

    eigen_part(0, qg, high_ref, low_ref, eig_in, eig_out, add)


def begin(owners, rows, rows_beside, kept_a, kept_g, lead, lead_beside, eig_in, eig_out):
    return pl.pallas_call(
        begin_kernel,
        in_specs=[SMEM] + [VMEM] * 8,
        out_specs=[VMEM] * 4,
        out_shape=[jax.ShapeDtypeStruct((D, D), BF16)] * 3 + [jax.ShapeDtypeStruct((HALF, D), F32)],
        scratch_shapes=[pltpu.VMEM((D, HALF), BF16)],
        compiler_params=params(24),
        cost_estimate=pl.CostEstimate(flops=7 * D**3, bytes_accessed=20 * D * D, transcendentals=0),
        name="begin",
    )(owners, rows, rows_beside, kept_a, kept_g, lead, lead_beside, eig_in, eig_out)


def finish_kernel(owners, high_ref, low_ref, qa, so_far, kept_g, rest, rest_beside, eig_in, eig_out,
                  out_ref, qg, back, final):
    gather(owners, 1, kept_g, HALF, rest, rest_beside, 0, QUARTER, qg)

    def add(row, col, got):
        back[:, col : col + 512] = so_far[:, col : col + 512] + got

    eigen_part(1, qg, high_ref, low_ref, eig_in, eig_out, add)
    high, low = split(back[...])
    both = jnp.concatenate([high, low], axis=0)
    for col in range(0, D, 512):
        got = lax.dot_general(both, qa[col : col + 512, :], (((1,), (1,)), ((), ())), preferred_element_type=F32)
        final[:, col : col + 512] = got[:HALF] + got[HALF:]
    for row in range(0, 256, 128):
        pieces = [final[at * 256 + row : at * 256 + row + 128, :].reshape(16, 1, 8, D) for at in range(2)]
        whole, tail = quantize(jnp.concatenate(pieces, axis=1).reshape(256, D))
        out_ref[2 * row : 2 * row + 256, :D] = whole
        out_ref[2 * row : 2 * row + 256, D:] = tail


def finish(owners, high, low, qa, so_far, kept_g, rest, rest_beside, eig_in, eig_out):
    return pl.pallas_call(
        finish_kernel,
        in_specs=[SMEM] + [VMEM] * 9,
        out_specs=VMEM,
        out_shape=jax.ShapeDtypeStruct((HALF, WIDE), I16),
        scratch_shapes=[pltpu.VMEM((D, HALF), BF16), pltpu.VMEM((HALF, D), F32), pltpu.VMEM((HALF, D), F32)],
        compiler_params=params(24),
        cost_estimate=pl.CostEstimate(flops=5 * D**3, bytes_accessed=10 * D * D, transcendentals=0),
        name="finish",
    )(owners, high, low, qa, so_far, kept_g, rest, rest_beside, eig_in, eig_out)


def after(x, earlier):
    return lax.optimization_barrier((x, earlier))[0]


def local(grads, basis_slots, owners, eig_in, eig_out):
    def across(x):
        return lax.ppermute(x, "zh", CORE_SWAP)

    def beside(x):
        return lax.ppermute(x, "core", CORE_SWAP)

    def everywhere(x):
        x = x.reshape(64, 8, WIDE)
        return lax.all_to_all(x, ("dp", "zh"), split_axis=0, concat_axis=0, tiled=True).reshape(HALF, WIDE)

    slots = basis_slots[0, 0]
    send = pick(owners, slots, beside(give(owners, slots)))
    lead = across(send)
    other = beside(after(slots, send))
    (send_rest,) = hold(rest_kernel, [(D, QUARTER)], owners, slots, other)
    rows = everywhere(after(quantize_rows(grads.reshape(HALF, D)), send_rest))
    rest = across(send_rest)
    rows_beside = beside(rows)
    kept_a, kept_g = hold(keep_kernel, [(D, D), (D, D)], owners, after(slots, rows), other)
    lead_beside = beside(lead)
    high, low, qa, so_far = begin(owners, rows, rows_beside, kept_a, kept_g, lead, lead_beside, eig_in, eig_out)
    rest_beside = beside(after(rest, so_far))
    out = finish(owners, high, low, qa, so_far, kept_g, rest, rest_beside, eig_in, eig_out)
    return restore_rows(everywhere(out)).reshape(64, 1, 8, D)


def solution(mesh):
    fine = Mesh(mesh.devices.reshape(32, 2, 2), ("dp", "zh", "core"))
    grad = ("zh", "core")
    return jax.shard_map(
        local,
        mesh=fine,
        in_specs=(
            P(None, grad, "dp", None),
            P("dp", grad, None, None, None),
            P("dp", None),
            P("dp", None),
            P("dp", None),
        ),
        out_specs=P(None, grad, "dp", None),
        check_vma=False,
    )
```

```python
import jax
import jax.numpy as jnp
from jax import lax
from jax.experimental import pallas as pl
from jax.experimental.pallas import tpu as pltpu
from jax.sharding import Mesh, PartitionSpec as P

D = 1024
HALF = 512
QUARTER = 256
LEAD = HALF + QUARTER
WIDE = D + 128
F32 = jnp.float32
BF16 = jnp.bfloat16
I16 = jnp.int16
ANY = pl.BlockSpec(memory_space=pl.ANY)
HBM = pl.BlockSpec(memory_space=pltpu.HBM)
VMEM = pl.BlockSpec(memory_space=pltpu.VMEM)
SMEM = pl.BlockSpec(memory_space=pltpu.SMEM)
CORE_SWAP = [(0, 1), (1, 0)]


def params(mebibytes):
    return pltpu.CompilerParams(vmem_limit_bytes=mebibytes * 1024 * 1024)


def basis_of(owners, module, side):
    flat = [owners[0, 0], owners[0, 1], owners[1, 0], owners[1, 1]]
    slot = []
    for k in range(4):
        total = jnp.int32(0)
        for j in range(k):
            total = total + (flat[j] == flat[k]).astype(jnp.int32)
        slot.append(total)
    first = module == 0
    owner = jnp.where(first, flat[side], flat[2 + side])
    return owner, jnp.where(first, slot[side], slot[2 + side])


def split(x):
    high = x.astype(BF16)
    return high, (x - high.astype(F32)).astype(BF16)


def quantize(x):
    most = jnp.maximum(jnp.max(jnp.abs(x), axis=1, keepdims=True), 1e-25)
    step = most * (1.0 / 32700.0)
    exponent = jnp.floor(jnp.log2(step))
    mantissa = jnp.clip(jnp.ceil(step * jnp.exp2(14.0 - exponent)), 1.0, 32767.0)
    scale = mantissa * jnp.exp2(exponent - 14.0)
    whole = jnp.clip(jnp.round(x * (1.0 / scale)), -32767.0, 32767.0)
    lane = lax.broadcasted_iota(jnp.int32, (x.shape[0], 128), 1)
    tail = jnp.where(lane < 64, exponent, mantissa)
    return whole.astype(jnp.int32).astype(I16), tail.astype(jnp.int32).astype(I16)


def scale_of(tail):
    tail = tail.astype(jnp.int32).astype(F32)
    return tail[:, 64:65] * jnp.exp2(tail[:, 0:1] - 14.0)


def quantize_kernel(x_ref, out_ref):
    whole, tail = quantize(x_ref[...])
    out_ref[:, :D] = whole
    out_ref[:, D:] = tail


def quantize_rows(x):
    rows = x.shape[0]
    return pl.pallas_call(
        quantize_kernel,
        grid=(4,),
        in_specs=[pl.BlockSpec((rows // 4, D), lambda i: (i, 0))],
        out_specs=pl.BlockSpec((rows // 4, WIDE), lambda i: (i, 0)),
        out_shape=jax.ShapeDtypeStruct((rows, WIDE), I16),
        compiler_params=params(12),
        cost_estimate=pl.CostEstimate(flops=0, bytes_accessed=rows * D * 6, transcendentals=0),
        name="quantize",
    )(x)


def restore_kernel(x_ref, out_ref):
    out_ref[...] = x_ref[:, :D].astype(jnp.int32).astype(F32) * scale_of(x_ref[:, D:])


def restore_rows(x):
    rows = x.shape[0]
    return pl.pallas_call(
        restore_kernel,
        grid=(2,),
        in_specs=[pl.BlockSpec((rows // 2, WIDE), lambda i: (i, 0))],
        out_specs=pl.BlockSpec((rows // 2, D), lambda i: (i, 0)),
        out_shape=jax.ShapeDtypeStruct((rows, D), F32),
        compiler_params=params(12),
        cost_estimate=pl.CostEstimate(flops=0, bytes_accessed=rows * D * 6, transcendentals=0),
        name="restore",
    )(x)


def place(owners, module, side, chip, core):
    owner, slot = basis_of(owners, module, side)
    return owner == 2 * chip + core, owner == 2 * chip + 1 - core, slot


def columns(ref, start, size):
    return ref.at[:, pl.ds(pl.multiple_of(start, size), size)]


def run_copies(items, sem):
    for act in ("start", "wait"):
        for at, (wanted, source, out) in enumerate(items):

            @pl.when(wanted)
            def _():
                getattr(pltpu.make_async_copy(source, out, sem.at[at]), act)()


def give_kernel(owners, slots, out, sem):
    chip, core = lax.axis_index("zh"), lax.axis_index("core")
    has_a, _, slot_a = place(owners, 1 - chip, 0, chip, core)
    has_g, _, slot_g = place(owners, 1 - chip, 1, chip, core)
    items = [
        (has_a, columns(slots.at[slot_a], (1 - core) * HALF, HALF), out.at[:, :HALF]),
        (has_g, columns(slots.at[slot_g], (1 - core) * QUARTER, QUARTER), out.at[:, HALF:]),
    ]
    run_copies(items, sem)


def give(owners, slots):
    return pl.pallas_call(
        give_kernel,
        in_specs=[SMEM, HBM],
        out_specs=VMEM,
        out_shape=jax.ShapeDtypeStruct((D, LEAD), BF16),
        scratch_shapes=[pltpu.SemaphoreType.DMA((2,))],
        compiler_params=params(8),
        cost_estimate=pl.CostEstimate(flops=0, bytes_accessed=3 * D * D, transcendentals=0),
        name="give",
    )(owners, slots)


def pick_kernel(owners, slots, given, out, sem):
    chip, core = lax.axis_index("zh"), lax.axis_index("core")
    has_a, beside_a, slot_a = place(owners, 1 - chip, 0, chip, core)
    has_g, beside_g, slot_g = place(owners, 1 - chip, 1, chip, core)
    items = [
        (has_a, columns(slots.at[slot_a], core * HALF, HALF), out.at[:, :HALF]),
        (beside_a, given.at[:, :HALF], out.at[:, :HALF]),
        (has_g, columns(slots.at[slot_g], core * QUARTER, QUARTER), out.at[:, HALF:]),
        (beside_g, given.at[:, HALF:], out.at[:, HALF:]),
    ]
    run_copies(items, sem)


def pick(owners, slots, given):
    return pl.pallas_call(
        pick_kernel,
        in_specs=[SMEM, HBM, ANY],
        out_specs=VMEM,
        out_shape=jax.ShapeDtypeStruct((D, LEAD), BF16),
        scratch_shapes=[pltpu.SemaphoreType.DMA((4,))],
        compiler_params=params(8),
        cost_estimate=pl.CostEstimate(flops=0, bytes_accessed=3 * D * D, transcendentals=0),
        name="pick",
    )(owners, slots, given)


def rest_kernel(owners, slots, other, out, sem):
    chip, core = lax.axis_index("zh"), lax.axis_index("core")
    has, beside, slot = place(owners, 1 - chip, 1, chip, core)
    items = []
    for wanted, source in ((has, slots), (beside, other)):
        items.append((wanted, columns(source.at[slot], HALF + core * QUARTER, QUARTER), out))
    run_copies(items, sem)


def keep_kernel(owners, slots, other, out_a, out_g, sem):
    chip, core = lax.axis_index("zh"), lax.axis_index("core")
    items = []
    for side, kept in enumerate((out_a, out_g)):
        has, beside, slot = place(owners, chip, side, chip, core)
        items += [(has, slots.at[slot], kept), (beside, other.at[slot], kept)]
    run_copies(items, sem)


def hold(kernel, shapes, owners, slots, other):
    return pl.pallas_call(
        kernel,
        in_specs=[SMEM, HBM, HBM],
        out_specs=[VMEM] * len(shapes),
        out_shape=[jax.ShapeDtypeStruct(shape, BF16) for shape in shapes],
        scratch_shapes=[pltpu.SemaphoreType.DMA((4,))],
        compiler_params=params(10),
        cost_estimate=pl.CostEstimate(flops=0, bytes_accessed=4 * D * D, transcendentals=0),
        name="hold",
    )(owners, slots, other)


def gather(owners, side, kept, kept_at, part, part_beside, part_at, size, out):
    chip, core = lax.axis_index("zh"), lax.axis_index("core")
    has, beside, _ = place(owners, chip, side, chip, core)

    @pl.when(has | beside)
    def _():
        out[...] = kept[:, kept_at : kept_at + 2 * size]

    @pl.when(jnp.logical_not(has | beside))
    def _():
        for source, at in ((part, core), (part_beside, 1 - core)):
            out[:, pl.ds(pl.multiple_of(at * size, size), size)] = source[:, part_at : part_at + size]


def rotate(rows, rows_beside, basis, high_ref, low_ref):
    core = lax.axis_index("core")
    for source, at in ((rows, core), (rows_beside, 1 - core)):
        for chip in range(2):
            block = source[...].astype(jnp.int32).astype(F32).reshape(32, 2, 8, WIDE)[:, chip].reshape(256, WIDE)
            scale = block[:, D + 64 : D + 65] * jnp.exp2(block[:, D : D + 1] - 14.0)
            high, low = split(block[:, :D])
            both = jnp.concatenate([high, low], axis=0)
            start = pl.multiple_of((2 * chip + at) * 256, 256)
            got = jnp.dot(both, basis[...], preferred_element_type=F32)
            got_high, got_low = split(((got[:256] + got[256:]) * scale).T)
            high_ref[:, pl.ds(start, 256)] = got_high
            low_ref[:, pl.ds(start, 256)] = got_low


def eigen_part(which, qg, high_ref, low_ref, eig_in, eig_out, add):
    chip, core = lax.axis_index("zh"), lax.axis_index("core")
    first = pl.multiple_of(core * 256, 256)
    eig_g = eig_out[pl.ds(chip, 1), which * HALF : (which + 1) * HALF]
    tops = jnp.concatenate([qg[pl.ds(first, 256), :], qg[pl.ds(first + HALF, 256), :]], axis=0)
    for row in range(0, D, 1024):
        both = jnp.concatenate([high_ref[row : row + 1024, :], low_ref[row : row + 1024, :]], axis=0)
        eigen = jnp.dot(both, qg[...], preferred_element_type=F32)
        eigen = eigen[:1024] + eigen[1024:]
        eig_a = jnp.broadcast_to(eig_in[pl.ds(chip, 1), row : row + 1024], (128, 1024)).T[:, 0:1]
        high, low = split(eigen / (eig_a * eig_g + 0.1))
        got = lax.dot_general(tops, high, (((1,), (1,)), ((), ())), preferred_element_type=F32)
        got = got + lax.dot_general(tops, low, (((1,), (1,)), ((), ())), preferred_element_type=F32)
        add(0, row, got)


def begin_kernel(owners, rows, rows_beside, kept_a, kept_g, lead, lead_beside, eig_in, eig_out,
                 high_ref, low_ref, qa, out_ref, qg):
    gather(owners, 0, kept_a, 0, lead, lead_beside, 0, HALF, qa)
    gather(owners, 1, kept_g, 0, lead, lead_beside, HALF, QUARTER, qg)
    rotate(rows, rows_beside, qa, high_ref, low_ref)

    def add(row, col, got):
        out_ref[:, col : col + 1024] = got

    eigen_part(0, qg, high_ref, low_ref, eig_in, eig_out, add)


def begin(owners, rows, rows_beside, kept_a, kept_g, lead, lead_beside, eig_in, eig_out):
    return pl.pallas_call(
        begin_kernel,
        in_specs=[SMEM] + [VMEM] * 8,
        out_specs=[VMEM] * 4,
        out_shape=[jax.ShapeDtypeStruct((D, D), BF16)] * 3 + [jax.ShapeDtypeStruct((HALF, D), F32)],
        scratch_shapes=[pltpu.VMEM((D, HALF), BF16)],
        compiler_params=params(24),
        cost_estimate=pl.CostEstimate(flops=7 * D**3, bytes_accessed=20 * D * D, transcendentals=0),
        name="begin",
    )(owners, rows, rows_beside, kept_a, kept_g, lead, lead_beside, eig_in, eig_out)


def finish_kernel(owners, high_ref, low_ref, qa, so_far, kept_g, rest, rest_beside, eig_in, eig_out,
                  out_ref, qg, back, final):
    gather(owners, 1, kept_g, HALF, rest, rest_beside, 0, QUARTER, qg)

    def add(row, col, got):
        back[:, col : col + 1024] = so_far[:, col : col + 1024] + got

    eigen_part(1, qg, high_ref, low_ref, eig_in, eig_out, add)
    high, low = split(back[...])
    both = jnp.concatenate([high, low], axis=0)
    for col in range(0, D, 512):
        got = lax.dot_general(both, qa[col : col + 512, :], (((1,), (1,)), ((), ())), preferred_element_type=F32)
        final[:, col : col + 512] = got[:HALF] + got[HALF:]
    for row in range(0, 256, 128):
        pieces = [final[at * 256 + row : at * 256 + row + 128, :].reshape(16, 1, 8, D) for at in range(2)]
        whole, tail = quantize(jnp.concatenate(pieces, axis=1).reshape(256, D))
        out_ref[2 * row : 2 * row + 256, :D] = whole
        out_ref[2 * row : 2 * row + 256, D:] = tail


def finish(owners, high, low, qa, so_far, kept_g, rest, rest_beside, eig_in, eig_out):
    return pl.pallas_call(
        finish_kernel,
        in_specs=[SMEM] + [VMEM] * 9,
        out_specs=VMEM,
        out_shape=jax.ShapeDtypeStruct((HALF, WIDE), I16),
        scratch_shapes=[pltpu.VMEM((D, HALF), BF16), pltpu.VMEM((HALF, D), F32), pltpu.VMEM((HALF, D), F32)],
        compiler_params=params(24),
        cost_estimate=pl.CostEstimate(flops=5 * D**3, bytes_accessed=10 * D * D, transcendentals=0),
        name="finish",
    )(owners, high, low, qa, so_far, kept_g, rest, rest_beside, eig_in, eig_out)


def after(x, earlier):
    return lax.optimization_barrier((x, earlier))[0]


def local(grads, basis_slots, owners, eig_in, eig_out):
    def across(x):
        return lax.ppermute(x, "zh", CORE_SWAP)

    def beside(x):
        return lax.ppermute(x, "core", CORE_SWAP)

    def everywhere(x):
        x = x.reshape(64, 8, WIDE)
        return lax.all_to_all(x, ("dp", "zh"), split_axis=0, concat_axis=0, tiled=True).reshape(HALF, WIDE)

    slots = basis_slots[0, 0]
    send = pick(owners, slots, beside(give(owners, slots)))
    lead = across(send)
    other = beside(after(slots, send))
    (send_rest,) = hold(rest_kernel, [(D, QUARTER)], owners, slots, other)
    rows = everywhere(after(quantize_rows(grads.reshape(HALF, D)), send_rest))
    rest = across(send_rest)
    rows_beside = beside(rows)
    kept_a, kept_g = hold(keep_kernel, [(D, D), (D, D)], owners, after(slots, rows), other)
    lead_beside = beside(lead)
    high, low, qa, so_far = begin(owners, rows, rows_beside, kept_a, kept_g, lead, lead_beside, eig_in, eig_out)
    rest_beside = beside(after(rest, so_far))
    out = finish(owners, high, low, qa, so_far, kept_g, rest, rest_beside, eig_in, eig_out)
    return restore_rows(everywhere(out)).reshape(64, 1, 8, D)


def solution(mesh):
    fine = Mesh(mesh.devices.reshape(32, 2, 2), ("dp", "zh", "core"))
    grad = ("zh", "core")
    return jax.shard_map(
        local,
        mesh=fine,
        in_specs=(
            P(None, grad, "dp", None),
            P("dp", grad, None, None, None),
            P("dp", None),
            P("dp", None),
            P("dp", None),
        ),
        out_specs=P(None, grad, "dp", None),
        check_vma=False,
    )
```

```python
import jax
import jax.numpy as jnp
from jax import lax
from jax.experimental import pallas as pl
from jax.experimental.pallas import tpu as pltpu
from jax.sharding import Mesh, PartitionSpec as P

D = 1024
HALF = 512
QUARTER = 256
LEAD = HALF + QUARTER
WIDE = D + 128
F32 = jnp.float32
BF16 = jnp.bfloat16
I16 = jnp.int16
ANY = pl.BlockSpec(memory_space=pl.ANY)
HBM = pl.BlockSpec(memory_space=pltpu.HBM)
VMEM = pl.BlockSpec(memory_space=pltpu.VMEM)
SMEM = pl.BlockSpec(memory_space=pltpu.SMEM)
CORE_SWAP = [(0, 1), (1, 0)]


def params(mebibytes):
    return pltpu.CompilerParams(vmem_limit_bytes=mebibytes * 1024 * 1024)


def basis_of(owners, module, side):
    flat = [owners[0, 0], owners[0, 1], owners[1, 0], owners[1, 1]]
    slot = []
    for k in range(4):
        total = jnp.int32(0)
        for j in range(k):
            total = total + (flat[j] == flat[k]).astype(jnp.int32)
        slot.append(total)
    first = module == 0
    owner = jnp.where(first, flat[side], flat[2 + side])
    return owner, jnp.where(first, slot[side], slot[2 + side])


def split(x):
    high = x.astype(BF16)
    return high, (x - high.astype(F32)).astype(BF16)


def quantize(x):
    most = jnp.maximum(jnp.max(jnp.abs(x), axis=1, keepdims=True), 1e-25)
    step = most * (1.0 / 32700.0)
    exponent = jnp.floor(jnp.log2(step))
    mantissa = jnp.clip(jnp.ceil(step * jnp.exp2(14.0 - exponent)), 1.0, 32767.0)
    scale = mantissa * jnp.exp2(exponent - 14.0)
    whole = jnp.clip(jnp.round(x * (1.0 / scale)), -32767.0, 32767.0)
    lane = lax.broadcasted_iota(jnp.int32, (x.shape[0], 128), 1)
    tail = jnp.where(lane < 64, exponent, mantissa)
    return whole.astype(jnp.int32).astype(I16), tail.astype(jnp.int32).astype(I16)


def scale_of(tail):
    tail = tail.astype(jnp.int32).astype(F32)
    return tail[:, 64:65] * jnp.exp2(tail[:, 0:1] - 14.0)


def quantize_kernel(x_ref, out_ref):
    whole, tail = quantize(x_ref[...])
    out_ref[:, :D] = whole
    out_ref[:, D:] = tail


def quantize_rows(x):
    rows = x.shape[0]
    return pl.pallas_call(
        quantize_kernel,
        grid=(4,),
        in_specs=[pl.BlockSpec((rows // 4, D), lambda i: (i, 0))],
        out_specs=pl.BlockSpec((rows // 4, WIDE), lambda i: (i, 0)),
        out_shape=jax.ShapeDtypeStruct((rows, WIDE), I16),
        compiler_params=params(12),
        cost_estimate=pl.CostEstimate(flops=0, bytes_accessed=rows * D * 6, transcendentals=0),
        name="quantize",
    )(x)


def restore_kernel(x_ref, out_ref):
    out_ref[...] = x_ref[:, :D].astype(jnp.int32).astype(F32) * scale_of(x_ref[:, D:])


def restore_rows(x):
    rows = x.shape[0]
    return pl.pallas_call(
        restore_kernel,
        grid=(2,),
        in_specs=[pl.BlockSpec((rows // 2, WIDE), lambda i: (i, 0))],
        out_specs=pl.BlockSpec((rows // 2, D), lambda i: (i, 0)),
        out_shape=jax.ShapeDtypeStruct((rows, D), F32),
        compiler_params=params(12),
        cost_estimate=pl.CostEstimate(flops=0, bytes_accessed=rows * D * 6, transcendentals=0),
        name="restore",
    )(x)


def place(owners, module, side, chip, core):
    owner, slot = basis_of(owners, module, side)
    return owner == 2 * chip + core, owner == 2 * chip + 1 - core, slot


def columns(ref, start, size):
    return ref.at[:, pl.ds(pl.multiple_of(start, size), size)]


def run_copies(items, sem):
    for act in ("start", "wait"):
        for at, (wanted, source, out) in enumerate(items):

            @pl.when(wanted)
            def _():
                getattr(pltpu.make_async_copy(source, out, sem.at[at]), act)()


def give_kernel(owners, slots, out, sem):
    chip, core = lax.axis_index("zh"), lax.axis_index("core")
    has_a, _, slot_a = place(owners, 1 - chip, 0, chip, core)
    has_g, _, slot_g = place(owners, 1 - chip, 1, chip, core)
    items = [
        (has_a, columns(slots.at[slot_a], (1 - core) * HALF, HALF), out.at[:, :HALF]),
        (has_g, columns(slots.at[slot_g], (1 - core) * QUARTER, QUARTER), out.at[:, HALF:]),
    ]
    run_copies(items, sem)


def give(owners, slots):
    return pl.pallas_call(
        give_kernel,
        in_specs=[SMEM, HBM],
        out_specs=VMEM,
        out_shape=jax.ShapeDtypeStruct((D, LEAD), BF16),
        scratch_shapes=[pltpu.SemaphoreType.DMA((2,))],
        compiler_params=params(8),
        cost_estimate=pl.CostEstimate(flops=0, bytes_accessed=3 * D * D, transcendentals=0),
        name="give",
    )(owners, slots)


def pick_kernel(owners, slots, given, out, sem):
    chip, core = lax.axis_index("zh"), lax.axis_index("core")
    has_a, beside_a, slot_a = place(owners, 1 - chip, 0, chip, core)
    has_g, beside_g, slot_g = place(owners, 1 - chip, 1, chip, core)
    items = [
        (has_a, columns(slots.at[slot_a], core * HALF, HALF), out.at[:, :HALF]),
        (beside_a, given.at[:, :HALF], out.at[:, :HALF]),
        (has_g, columns(slots.at[slot_g], core * QUARTER, QUARTER), out.at[:, HALF:]),
        (beside_g, given.at[:, HALF:], out.at[:, HALF:]),
    ]
    run_copies(items, sem)


def pick(owners, slots, given):
    return pl.pallas_call(
        pick_kernel,
        in_specs=[SMEM, HBM, ANY],
        out_specs=VMEM,
        out_shape=jax.ShapeDtypeStruct((D, LEAD), BF16),
        scratch_shapes=[pltpu.SemaphoreType.DMA((4,))],
        compiler_params=params(8),
        cost_estimate=pl.CostEstimate(flops=0, bytes_accessed=3 * D * D, transcendentals=0),
        name="pick",
    )(owners, slots, given)


def rest_kernel(owners, slots, other, out, sem):
    chip, core = lax.axis_index("zh"), lax.axis_index("core")
    has, beside, slot = place(owners, 1 - chip, 1, chip, core)
    items = []
    for wanted, source in ((has, slots), (beside, other)):
        items.append((wanted, columns(source.at[slot], HALF + core * QUARTER, QUARTER), out))
    run_copies(items, sem)


def keep_kernel(owners, slots, other, out_a, out_g, sem):
    chip, core = lax.axis_index("zh"), lax.axis_index("core")
    items = []
    for side, kept in enumerate((out_a, out_g)):
        has, beside, slot = place(owners, chip, side, chip, core)
        items += [(has, slots.at[slot], kept), (beside, other.at[slot], kept)]
    run_copies(items, sem)


def hold(kernel, shapes, owners, slots, other):
    return pl.pallas_call(
        kernel,
        in_specs=[SMEM, HBM, HBM],
        out_specs=[VMEM] * len(shapes),
        out_shape=[jax.ShapeDtypeStruct(shape, BF16) for shape in shapes],
        scratch_shapes=[pltpu.SemaphoreType.DMA((4,))],
        compiler_params=params(48),
        cost_estimate=pl.CostEstimate(flops=0, bytes_accessed=4 * D * D, transcendentals=0),
        name="hold",
    )(owners, slots, other)


def gather(owners, side, kept, kept_at, part, part_beside, part_at, size, out):
    chip, core = lax.axis_index("zh"), lax.axis_index("core")
    has, beside, _ = place(owners, chip, side, chip, core)

    @pl.when(has | beside)
    def _():
        out[...] = kept[:, kept_at : kept_at + 2 * size]

    @pl.when(jnp.logical_not(has | beside))
    def _():
        for source, at in ((part, core), (part_beside, 1 - core)):
            out[:, pl.ds(pl.multiple_of(at * size, size), size)] = source[:, part_at : part_at + size]


def rotate(rows, rows_beside, basis, high_ref, low_ref):
    core = lax.axis_index("core")
    for source, at in ((rows, core), (rows_beside, 1 - core)):
        for chip in range(2):
            block = source[...].astype(jnp.int32).astype(F32).reshape(32, 2, 8, WIDE)[:, chip].reshape(256, WIDE)
            scale = block[:, D + 64 : D + 65] * jnp.exp2(block[:, D : D + 1] - 14.0)
            high, low = split(block[:, :D])
            both = jnp.concatenate([high, low], axis=0)
            start = pl.multiple_of((2 * chip + at) * 256, 256)
            got = jnp.dot(both, basis[...], preferred_element_type=F32)
            got_high, got_low = split(((got[:256] + got[256:]) * scale).T)
            high_ref[:, pl.ds(start, 256)] = got_high
            low_ref[:, pl.ds(start, 256)] = got_low


def eigen_part(which, qg, high_ref, low_ref, eig_in, eig_out, add):
    chip, core = lax.axis_index("zh"), lax.axis_index("core")
    first = pl.multiple_of(core * 256, 256)
    eig_g = eig_out[pl.ds(chip, 1), which * HALF : (which + 1) * HALF]
    tops = jnp.concatenate([qg[pl.ds(first, 256), :], qg[pl.ds(first + HALF, 256), :]], axis=0)
    for row in range(0, D, 1024):
        both = jnp.concatenate([high_ref[row : row + 1024, :], low_ref[row : row + 1024, :]], axis=0)
        eigen = jnp.dot(both, qg[...], preferred_element_type=F32)
        eigen = eigen[:1024] + eigen[1024:]
        eig_a = jnp.broadcast_to(eig_in[pl.ds(chip, 1), row : row + 1024], (128, 1024)).T[:, 0:1]
        high, low = split(eigen / (eig_a * eig_g + 0.1))
        got = lax.dot_general(tops, high, (((1,), (1,)), ((), ())), preferred_element_type=F32)
        got = got + lax.dot_general(tops, low, (((1,), (1,)), ((), ())), preferred_element_type=F32)
        add(0, row, got)


def begin_kernel(owners, rows, rows_beside, kept_a, kept_g, lead, lead_beside, eig_in, eig_out,
                 high_ref, low_ref, qa, out_ref, qg):
    gather(owners, 0, kept_a, 0, lead, lead_beside, 0, HALF, qa)
    gather(owners, 1, kept_g, 0, lead, lead_beside, HALF, QUARTER, qg)
    rotate(rows, rows_beside, qa, high_ref, low_ref)

    def add(row, col, got):
        out_ref[:, col : col + 1024] = got

    eigen_part(0, qg, high_ref, low_ref, eig_in, eig_out, add)


def begin(owners, rows, rows_beside, kept_a, kept_g, lead, lead_beside, eig_in, eig_out):
    return pl.pallas_call(
        begin_kernel,
        in_specs=[SMEM] + [VMEM] * 8,
        out_specs=[VMEM] * 4,
        out_shape=[jax.ShapeDtypeStruct((D, D), BF16)] * 3 + [jax.ShapeDtypeStruct((HALF, D), F32)],
        scratch_shapes=[pltpu.VMEM((D, HALF), BF16)],
        compiler_params=params(24),
        cost_estimate=pl.CostEstimate(flops=7 * D**3, bytes_accessed=20 * D * D, transcendentals=0),
        name="begin",
    )(owners, rows, rows_beside, kept_a, kept_g, lead, lead_beside, eig_in, eig_out)


def finish_kernel(owners, high_ref, low_ref, qa, so_far, kept_g, rest, rest_beside, eig_in, eig_out,
                  out_ref, qg, back, final):
    gather(owners, 1, kept_g, HALF, rest, rest_beside, 0, QUARTER, qg)

    def add(row, col, got):
        back[:, col : col + 1024] = so_far[:, col : col + 1024] + got

    eigen_part(1, qg, high_ref, low_ref, eig_in, eig_out, add)
    high, low = split(back[...])
    both = jnp.concatenate([high, low], axis=0)
    for col in range(0, D, 512):
        got = lax.dot_general(both, qa[col : col + 512, :], (((1,), (1,)), ((), ())), preferred_element_type=F32)
        final[:, col : col + 512] = got[:HALF] + got[HALF:]
    for row in range(0, 256, 128):
        pieces = [final[at * 256 + row : at * 256 + row + 128, :].reshape(16, 1, 8, D) for at in range(2)]
        whole, tail = quantize(jnp.concatenate(pieces, axis=1).reshape(256, D))
        out_ref[2 * row : 2 * row + 256, :D] = whole
        out_ref[2 * row : 2 * row + 256, D:] = tail


def finish(owners, high, low, qa, so_far, kept_g, rest, rest_beside, eig_in, eig_out):
    return pl.pallas_call(
        finish_kernel,
        in_specs=[SMEM] + [VMEM] * 9,
        out_specs=VMEM,
        out_shape=jax.ShapeDtypeStruct((HALF, WIDE), I16),
        scratch_shapes=[pltpu.VMEM((D, HALF), BF16), pltpu.VMEM((HALF, D), F32), pltpu.VMEM((HALF, D), F32)],
        compiler_params=params(24),
        cost_estimate=pl.CostEstimate(flops=5 * D**3, bytes_accessed=10 * D * D, transcendentals=0),
        name="finish",
    )(owners, high, low, qa, so_far, kept_g, rest, rest_beside, eig_in, eig_out)


def after(x, earlier):
    return lax.optimization_barrier((x, earlier))[0]


def local(grads, basis_slots, owners, eig_in, eig_out):
    def across(x):
        return lax.ppermute(x, "zh", CORE_SWAP)

    def beside(x):
        return lax.ppermute(x, "core", CORE_SWAP)

    def everywhere(x):
        x = x.reshape(64, 8, WIDE)
        return lax.all_to_all(x, ("dp", "zh"), split_axis=0, concat_axis=0, tiled=True).reshape(HALF, WIDE)

    slots = basis_slots[0, 0]
    send = pick(owners, slots, beside(give(owners, slots)))
    lead = across(send)
    other = beside(after(slots, send))
    (send_rest,) = hold(rest_kernel, [(D, QUARTER)], owners, slots, other)
    rows = everywhere(after(quantize_rows(grads.reshape(HALF, D)), send_rest))
    rest = across(send_rest)
    rows_beside = beside(rows)
    kept_a, kept_g = hold(keep_kernel, [(D, D), (D, D)], owners, after(slots, rows), other)
    lead_beside = beside(lead)
    high, low, qa, so_far = begin(owners, rows, rows_beside, kept_a, kept_g, lead, lead_beside, eig_in, eig_out)
    rest_beside = beside(after(rest, so_far))
    out = finish(owners, high, low, qa, so_far, kept_g, rest, rest_beside, eig_in, eig_out)
    return restore_rows(everywhere(out)).reshape(64, 1, 8, D)


def solution(mesh):
    fine = Mesh(mesh.devices.reshape(32, 2, 2), ("dp", "zh", "core"))
    grad = ("zh", "core")
    return jax.shard_map(
        local,
        mesh=fine,
        in_specs=(
            P(None, grad, "dp", None),
            P("dp", grad, None, None, None),
            P("dp", None),
            P("dp", None),
            P("dp", None),
        ),
        out_specs=P(None, grad, "dp", None),
        check_vma=False,
    )
```
